32 devices in a mesh: comp: 2 (over core), tile: 8 (over z, y), lev: 2 (over x).
Axes of the slice: x: 2, y: 2, z: 4, core: 2. Of those that a mesh axis runs over, the one named last changes fastest.
Arguments:
- climate_departure: bfloat16 [128, 64, 1024], P(('comp', 'lev'), None, 'tile'), may hold values from -6 to 6
- spread_rate: float32 [64, 1024], P(None, 'tile'), may hold values from 0.02 to 0.15
- advection_fraction: float32 [128], P(('comp', 'lev')), may hold values from 0.05 to 0.3
- blend_kernel_excess: bfloat16 [128, 128], P(('comp', 'lev')), may hold values from -0.5 to 0.5
- layer_emission_share: bfloat16 [4, 128], replicated, may hold values from -0.5 to 0.5
- link_coupling_submatrix: bfloat16 [8, 16, 128, 128], P('tile'), may hold values from -0.5 to 0.5
- link_provider_group: int32 [8, 16], P('tile'), may hold values from 0 to 7, as said below
- occupied_link_total: int32 [8], P('tile'), may hold values from 4 to 16, as said below
- water_top_departure: float32 [64, 1024], P(None, 'tile'), may hold values from -6 to 6
- pond_spread_rate: float32 [64, 1024], P(None, 'tile'), may hold values from 0.02 to 0.2
- water_reaction: float32 [4], replicated, may hold values from 0.1 to 0.5
Outputs:
- stepped_climate: bfloat16 [128, 64, 1024], P(('comp', 'lev'), None, 'tile')
- water_top_later: float32 [64, 1024], P(None, 'tile')
The draws below stay inside these ranges and needn't reach their ends.
Inputs may be any that keep to these rules, and one draw needn't show every extreme that they name: `link_provider_group`: slots b >= occupied_link_total[t] of ocean tile t are unused. Slot 0 of ocean tile t names atmosphere tile t. Every slot of ocean tile t names a tile at most 3 tiles away from t along the periodic circle of tiles. `occupied_link_total`: some ocean tile uses all 16 slots.
All inputs are finite; a program needn't handle non-finite values.
Results may differ from the reference program's by a relative error of at most 0.0051.
Values may be sent and summed in bfloat16 or wider, within the bound.
A program may use at most 64 MiB of HBM per device.

```python
import math
import jax
import jax.numpy as jnp
from jax import lax

LEVELS = 128
NORTH_SOUTH_SPAN = 64
CELL_DEV = 128
OCEAN_DEV = 128
FIELDS = 4
MOST_BLOCKS = 16
REACH = 3
CELLS = 1024
WATER_GRID_SIZE = 1024
OCEAN_TILES = 8
N_TILE = 8


def draw_link_provider_group(key, part):
    key = jax.random.fold_in(key, 11)
    offsets = jax.random.randint(key, (OCEAN_TILES, MOST_BLOCKS), -REACH, REACH + 1).astype(jnp.int32)
    tiles = jnp.arange(OCEAN_TILES, dtype=jnp.int32)
    cycle = tiles % (2 * REACH)
    nonzero = jnp.where(cycle < REACH, cycle - REACH, cycle - REACH + 1).astype(jnp.int32)
    offsets = offsets.at[:, 0].set(0)
    offsets = offsets.at[:, 1].set(nonzero)
    return ((tiles[:, None] + offsets) % OCEAN_TILES).astype(jnp.int32)


def draw_occupied_link_total(key, part):
    key = jax.random.fold_in(key, 12)
    count_key, pick_key = jax.random.split(key)
    lowest = max(2, MOST_BLOCKS // 4)
    counts = jax.random.randint(count_key, (OCEAN_TILES,), lowest, MOST_BLOCKS + 1).astype(jnp.int32)
    chosen = jax.random.randint(pick_key, (), 0, OCEAN_TILES)
    return jnp.where(jnp.arange(OCEAN_TILES) == chosen, MOST_BLOCKS, counts).astype(jnp.int32)


def block_levels(key, dims, shards, smallest, top_value):
    def one(dim, blocks):
        draws = jax.random.uniform(jax.random.fold_in(jax.random.fold_in(key, 6), dim), (blocks,), jnp.float32, smallest / len(shards), top_value / len(shards))
        return jnp.repeat(jnp.exp(draws), dims[dim] // blocks).reshape((-1,) + (1,) * (len(dims) - dim - 1))

    loudness = one(*shards[0])
    for cut in shards[1:]:
        loudness = loudness * one(*cut)
    return loudness


def bell_draw(rng, extent, scale, most, pieces=(), kind=jnp.bfloat16):
    values = jax.random.normal(rng, extent, jnp.float32) * scale
    if len(pieces) > 0:
        values = block_levels(rng, extent, pieces, -0.22, 0.18) * values
    return jnp.clip(values, min=-most, max=most).astype(kind)


def setup_inputs(seed: int = 0) -> dict:
    keys = jax.random.split(jax.random.key(seed), 12)
    return {
        "climate_departure": bell_draw(keys[0], (LEVELS, NORTH_SOUTH_SPAN, CELLS), 1.0, 6.0, ((0, 4), (2, 8))),
        "spread_rate": jnp.clip(jnp.exp(math.log(0.15) - 2.014903 * jax.random.uniform(keys[1], (NORTH_SOUTH_SPAN, CELLS), jnp.float32) ** block_levels(keys[1], (NORTH_SOUTH_SPAN, CELLS), ((1, 8),), -0.2, 0.2)), 0.02, 0.15),
        "advection_fraction": jnp.clip(jnp.exp(math.log(0.3) - 1.7917595 * jax.random.uniform(keys[2], (LEVELS,), jnp.float32) ** block_levels(keys[2], (LEVELS,), ((0, 4),), -0.2, 0.2)), 0.05, 0.3),
        "blend_kernel_excess": bell_draw(keys[3], (LEVELS, LEVELS), LEVELS ** -0.5, 0.5, ((0, 4),)),
        "layer_emission_share": bell_draw(keys[4], (FIELDS, LEVELS), LEVELS ** -0.5, 0.5),
        "link_coupling_submatrix": bell_draw(keys[5], (OCEAN_TILES, MOST_BLOCKS, CELL_DEV, OCEAN_DEV), CELL_DEV ** -0.5, 0.5, ((0, 8),)),
        "link_provider_group": draw_link_provider_group(jax.random.fold_in(keys[11], 71), 0),
        "occupied_link_total": draw_occupied_link_total(jax.random.fold_in(keys[11], 71), 0),
        "water_top_departure": bell_draw(keys[8], (NORTH_SOUTH_SPAN, WATER_GRID_SIZE), 1.0, 6.0, ((1, 8),), jnp.float32),
        "pond_spread_rate": jnp.clip(jnp.exp(math.log(0.2) - 2.3025851 * jax.random.uniform(keys[9], (NORTH_SOUTH_SPAN, WATER_GRID_SIZE), jnp.float32) ** block_levels(keys[9], (NORTH_SOUTH_SPAN, WATER_GRID_SIZE), ((1, 8),), -0.2, 0.2)), 0.02, 0.2),
        "water_reaction": jnp.clip(jax.random.uniform(keys[10], (FIELDS,), jnp.float32, 0.1, 0.5), 0.1, 0.5),
    }


def reference(climate_departure, spread_rate, advection_fraction, blend_kernel_excess, layer_emission_share, link_coupling_submatrix, link_provider_group, occupied_link_total, water_top_departure, pond_spread_rate, water_reaction):
    field = climate_departure.astype(jnp.float32)
    padded = jnp.pad(field, ((0, 0), (1, 1), (0, 0)))
    west = jnp.roll(field, 1, axis=2)
    east = jnp.roll(field, -1, axis=2)
    lap = padded[:, 2:, :] + padded[:, :-2, :] + east + west - 4.0 * field
    advected = (field + spread_rate[None] * lap - advection_fraction[:, None, None] * (field - west)).astype(jnp.bfloat16)
    flat = advected.reshape(LEVELS, -1)
    stepped_climate = (advected.astype(jnp.float32) + jnp.dot(blend_kernel_excess, flat, preferred_element_type=jnp.float32).reshape(advected.shape)).astype(jnp.bfloat16)
    flux = jnp.dot(layer_emission_share, flat, preferred_element_type=jnp.float32).astype(jnp.bfloat16)
    flux = flux.reshape(FIELDS, NORTH_SOUTH_SPAN, N_TILE, CELL_DEV)

    def one_tile(items):
        sources, count, weight = items
        blocks = jnp.take(flux, sources, axis=2).astype(jnp.float32)
        live = (jnp.arange(MOST_BLOCKS) < count).astype(jnp.float32)
        blocks = blocks * live[None, None, :, None]
        return jnp.einsum("frbc,bco->fro", blocks, weight.astype(jnp.float32), precision=lax.Precision.HIGHEST)

    per_tile = lax.map(one_tile, (link_provider_group, occupied_link_total, link_coupling_submatrix))
    ocean_flux = jnp.transpose(per_tile, (1, 2, 0, 3)).reshape(FIELDS, NORTH_SOUTH_SPAN, WATER_GRID_SIZE)
    pond_halo_array = jnp.pad(water_top_departure, ((1, 1), (0, 0)))
    pond_second_derivative_sum = pond_halo_array[2:] + pond_halo_array[:-2] + jnp.roll(water_top_departure, 1, axis=1) + jnp.roll(water_top_departure, -1, axis=1) - 4.0 * water_top_departure
    bottom_layer_push = jnp.sum(water_reaction[:, None, None] * ocean_flux, axis=0)
    water_top_later = water_top_departure + pond_spread_rate * pond_second_derivative_sum + bottom_layer_push
    return stepped_climate, water_top_later
```

```python
import functools

import jax
import jax.numpy as jnp
from jax import lax
from jax.experimental import pallas as pl
from jax.experimental.pallas import tpu as pltpu
from jax.sharding import PartitionSpec as P

REACH_MOST = 8
PIECES = 8
CHUNKS = 4
MESH = pl.DeviceIdType.MESH
F32 = jnp.float32
BF16 = jnp.bfloat16


def iota(shape, dim):
    return lax.broadcasted_iota(jnp.int32, shape, dim)


def kernel(
    n_comp,
    n_tile,
    n_lev,
    state,
    spread,
    fraction,
    blend,
    share,
    weight,
    source,
    used,
    water,
    pond,
    reaction,
    out_state,
    out_water,
    edge,
    edge_in,
    turned,
    gathered,
    mixed,
    emission,
    part,
    part_in,
    near,
    water_in,
    ocean,
    ocean_in,
    edge_send,
    edge_recv,
    lev_send,
    lev_recv,
    comp_send,
    comp_recv,
    part_send,
    part_recv,
    near_send,
    near_recv,
    water_send,
    water_recv,
    ocean_send,
    ocean_recv,
):
    depth, rows, width = state.shape
    levels = blend.shape[1]
    fields = share.shape[0]
    most = weight.shape[1]
    reach = min(REACH_MOST, (n_tile - 1) // 2)
    half = rows // n_comp
    span = rows // CHUNKS
    per_piece = depth // PIECES
    piece_rows = per_piece * rows

    comp = lax.axis_index("comp")
    tile = lax.axis_index("tile")
    lev = lax.axis_index("lev")
    block = comp * n_lev + lev
    half_at = pl.multiple_of(comp * half, half)

    def at(dc=0, dt=0, dl=0):
        return (
            lax.rem(comp + dc, n_comp),
            lax.rem(tile + dt + n_tile, n_tile),
            lax.rem(lev + dl, n_lev),
        )

    group = [(dc, dl) for dc in range(n_comp) for dl in range(n_lev) if dc or dl]
    offsets = [o for d in range(1, reach + 1) for o in (d, -d)]

    def remote(src, dst, send, recv, device):
        copy = pltpu.make_async_remote_copy(
            src_ref=src,
            dst_ref=dst,
            send_sem=send,
            recv_sem=recv,
            device_id=device,
            device_id_type=MESH,
        )
        return copy

    barrier = pltpu.get_barrier_semaphore()
    for dc, dl in group:
        pl.semaphore_signal(barrier, inc=1, device_id=at(dc, 0, dl), device_id_type=MESH)
    for o in offsets:
        pl.semaphore_signal(barrier, inc=1, device_id=at(0, o, 0), device_id_type=MESH)

    row16, col16 = iota((16, width), 0), iota((16, width), 1)
    packed = jnp.zeros((16, piece_rows), F32)
    for p in range(PIECES):
        pick = ((row16 == p) & (col16 == width - 1)) | ((row16 == PIECES + p) & (col16 == 0))
        cells = state[p * per_piece : (p + 1) * per_piece].reshape(piece_rows, width)
        packed += lax.dot_general(
            jnp.where(pick, 1.0, 0.0).astype(BF16),
            cells,
            (((1,), (1,)), ((), ())),
            preferred_element_type=F32,
        )
    edge[...] = packed.astype(BF16)

    own = iota((depth, levels), 1) == iota((depth, levels), 0) + block * depth
    own_share = lax.dot_general(
        jnp.where(own, 1.0, 0.0).astype(BF16),
        share[...],
        (((1,), (1,)), ((), ())),
        preferred_element_type=F32,
    )
    total = jnp.zeros((depth, 1), F32)
    for f in range(fields):
        total += reaction[f] * own_share[:, f : f + 1]
    emission[...] = jnp.broadcast_to(total, (depth, width))

    pl.semaphore_wait(barrier, len(group) + len(offsets))

    edge_copies = []
    for s, o in enumerate((1, -1)):
        copy = remote(edge, edge_in.at[s], edge_send.at[s], edge_recv.at[s], at(0, o, 0))
        copy.start()
        edge_copies.append(copy)
    for copy in edge_copies:
        copy.wait_recv()

    sides = jnp.concatenate([edge_in[0], edge_in[1]], axis=0).astype(F32)
    sides = sides.T.astype(BF16)
    row32, col32 = iota((32, width), 0), iota((32, width), 1)
    lat, lon = iota((rows, width), 0), iota((rows, width), 1)
    rate = spread[...]

    def one_piece(p, emitted):
        place = ((row32 == p) & (col32 == 0)) | (
            (row32 == 16 + PIECES + p) & (col32 == width - 1)
        )
        border = jnp.dot(
            sides, jnp.where(place, 1.0, 0.0).astype(BF16), preferred_element_type=F32
        )
        for q in range(per_piece):
            k = p * per_piece + q
            field = state[k].astype(F32)
            rim = border[q * rows : (q + 1) * rows]
            west = jnp.where(lon == 0, rim, pltpu.roll(field, 1, 1))
            east = jnp.where(lon == width - 1, rim, pltpu.roll(field, width - 1, 1))
            above = jnp.where(lat == rows - 1, 0.0, pltpu.roll(field, rows - 1, 0))
            below = jnp.where(lat == 0, 0.0, pltpu.roll(field, 1, 0))
            lap = above + below + east + west - 4.0 * field
            moved = field + rate * lap - fraction[k] * (field - west)
            moved = moved.astype(BF16).astype(F32)
            turned[pl.ds(k, rows, stride=depth), :] = moved
            emitted = emitted + emission[pl.ds(k, 1), :] * moved
        return emitted

    part[...] = lax.fori_loop(0, PIECES, one_piece, jnp.zeros((rows, width), F32))

    copies = []

    part_copies = []
    for i, (dc, dl) in enumerate(group):
        device = at(dc, 0, dl)
        begin = pl.multiple_of(device[0] * half, half)
        copy = remote(
            part.at[pl.ds(begin, half)], part_in.at[i], part_send.at[i], part_recv.at[i], device
        )
        copy.start()
        part_copies.append(copy)

    lev_copies, comp_copies = {}, {}
    for i in range(CHUNKS):
        lines = turned[i * span * depth : (i + 1) * span * depth]
        gathered[block, i * span : (i + 1) * span] = lines.astype(BF16).reshape(span, depth, width)
        mine = gathered.at[block, pl.ds(i * span, span)]
        for dl in range(1, n_lev):
            copy = remote(
                mine, mine, lev_send.at[dl - 1, i], lev_recv.at[dl - 1, i], at(0, 0, dl)
            )
            copy.start()
            lev_copies[dl, i] = copy
        for dc in range(1, n_comp):
            copy = remote(
                mine, mine, comp_send.at[dc - 1, 0, i], comp_recv.at[dc - 1, 0, i], at(dc, 0, 0)
            )
            copy.start()
            comp_copies[dc, 0, i] = copy

    water_copies = []
    for s, o in enumerate((1, -1)):
        copy = remote(
            water.at[pl.ds(half_at, half)],
            water_in.at[s],
            water_send.at[s],
            water_recv.at[s],
            at(0, o, 0),
        )
        copy.start()
        water_copies.append(copy)

    for copy in part_copies:
        copy.wait_recv()
    flux = part[pl.ds(half_at, half), :]
    for i in range(len(group)):
        flux += part_in[i]
    near[reach] = flux.astype(BF16)
    near_copies = []
    for i, o in enumerate(offsets):
        copy = remote(
            near.at[reach], near.at[reach - o], near_send.at[i], near_recv.at[i], at(0, o, 0)
        )
        copy.start()
        near_copies.append(copy)

    def relay(i):
        for dl in range(1, n_lev):
            lev_copies[dl, i].wait_recv()
            origin = comp * n_lev + lax.rem(lev - dl + n_lev, n_lev)
            theirs = gathered.at[origin, pl.ds(i * span, span)]
            for dc in range(1, n_comp):
                copy = remote(
                    theirs,
                    theirs,
                    comp_send.at[dc - 1, dl, i],
                    comp_recv.at[dc - 1, dl, i],
                    at(dc, 0, 0),
                )
                copy.start()
                comp_copies[dc, dl, i] = copy

    def mix(i):
        for dc in range(1, n_comp):
            for dl in range(n_lev):
                comp_copies[dc, dl, i].wait_recv()
        factor = blend[...]
        for r in range(i * span, (i + 1) * span):
            column = gathered[:, r].reshape(levels, width)
            new = jnp.dot(factor, column, preferred_element_type=F32)
            new += gathered[block, r].astype(F32)
            mixed[pl.ds(r, depth, stride=rows), :] = new
        done = mixed[...].reshape(depth, rows, width)[:, i * span : (i + 1) * span]
        out_state[:, i * span : (i + 1) * span, :] = done.astype(BF16)

    def remap():
        for copy in near_copies:
            copy.wait_recv()
        for copy in water_copies:
            copy.wait_recv()
        picked = []
        for b in range(most):
            slot = lax.rem(source[0, b] - tile + reach + 2 * n_tile, n_tile)
            slot = jnp.minimum(slot, 2 * reach)
            live = jnp.where(b < used[0], 1.0, 0.0).astype(F32)
            picked.append((near[slot].astype(F32) * live).astype(BF16))
        push = jnp.dot(
            jnp.concatenate(picked, axis=1),
            weight[0].reshape(most * width, width),
            preferred_element_type=F32,
        )
        top = water[...]
        above = jnp.where(lat == rows - 1, 0.0, pltpu.roll(top, rows - 1, 0))
        below = jnp.where(lat == 0, 0.0, pltpu.roll(top, 1, 0))
        ocean[...] = above + below - 4.0 * top
        mine = water[pl.ds(half_at, half), :]
        at_lon = iota((half, width), 1)
        west = jnp.where(at_lon == 0, pltpu.roll(water_in[0], 1, 1), pltpu.roll(mine, 1, 1))
        east = jnp.where(
            at_lon == width - 1,
            pltpu.roll(water_in[1], width - 1, 1),
            pltpu.roll(mine, width - 1, 1),
        )
        bend = ocean[pl.ds(half_at, half), :] + west + east
        later = mine + pond[pl.ds(half_at, half), :] * bend + push
        ocean_in[0] = later
        out_water[pl.ds(half_at, half), :] = later
        sent = []
        for dc in range(1, n_comp):
            copy = remote(
                ocean_in.at[0],
                ocean_in.at[dc],
                ocean_send.at[dc - 1],
                ocean_recv.at[dc - 1],
                at(dc, 0, 0),
            )
            copy.start()
            sent.append(copy)
        return sent

    relay(0)
    relay(1)
    mix(0)
    ocean_copies = remap()
    for i in range(2, CHUNKS):
        relay(i)
        mix(i - 1)
    mix(CHUNKS - 1)
    for dc in range(1, n_comp):
        ocean_copies[dc - 1].wait_recv()
        begin = pl.multiple_of(lax.rem(comp - dc + n_comp, n_comp) * half, half)
        out_water[pl.ds(begin, half), :] = ocean_in[dc]

    for copy in edge_copies + part_copies + water_copies + near_copies + ocean_copies:
        copy.wait_send()
    for copy in list(lev_copies.values()) + list(comp_copies.values()):
        copy.wait_send()


def solution(mesh):
    n_comp, n_tile, n_lev = (mesh.shape[a] for a in ("comp", "tile", "lev"))

    def on_device(*args):
        state, spread, fraction, blend, share, weight, source, used, water, pond, reaction = args
        depth, rows, width = state.shape
        reach = min(REACH_MOST, (n_tile - 1) // 2)
        half = rows // n_comp
        peers = n_comp * n_lev - 1
        dma = pltpu.SemaphoreType.DMA
        vmem = pl.BlockSpec(memory_space=pltpu.VMEM)
        smem = pl.BlockSpec(memory_space=pltpu.SMEM)
        piece = depth * rows // PIECES
        return pl.pallas_call(
            functools.partial(kernel, n_comp, n_tile, n_lev),
            out_shape=(
                jax.ShapeDtypeStruct(state.shape, state.dtype),
                jax.ShapeDtypeStruct(water.shape, water.dtype),
            ),
            in_specs=[vmem, vmem, smem, vmem, vmem, vmem, smem, smem, vmem, vmem, smem],
            out_specs=(vmem, vmem),
            scratch_shapes=[
                pltpu.VMEM((16, piece), BF16),
                pltpu.VMEM((2, 16, piece), BF16),
                pltpu.VMEM((rows * depth, width), F32),
                pltpu.VMEM((n_comp * n_lev, rows, depth, width), BF16),
                pltpu.VMEM((depth * rows, width), F32),
                pltpu.VMEM((depth, width), F32),
                pltpu.VMEM((rows, width), F32),
                pltpu.VMEM((peers, half, width), F32),
                pltpu.VMEM((2 * reach + 1, half, width), BF16),
                pltpu.VMEM((2, half, width), F32),
                pltpu.VMEM((rows, width), F32),
                pltpu.VMEM((n_comp, half, width), F32),
                dma((2,)),
                dma((2,)),
                dma((n_lev - 1, CHUNKS)),
                dma((n_lev - 1, CHUNKS)),
                dma((n_comp - 1, n_lev, CHUNKS)),
                dma((n_comp - 1, n_lev, CHUNKS)),
                dma((peers,)),
                dma((peers,)),
                dma((2 * reach,)),
                dma((2 * reach,)),
                dma((2,)),
                dma((2,)),
                dma((n_comp - 1,)),
                dma((n_comp - 1,)),
            ],
            compiler_params=pltpu.CompilerParams(
                collective_id=0, has_side_effects=True, vmem_limit_bytes=32 * 1024 * 1024
            ),
            cost_estimate=pl.CostEstimate(
                flops=200_000_000, bytes_accessed=2_000_000, transcendentals=0
            ),
        )(state, spread, fraction, blend, share, weight, source, used, water, pond, reaction)

    in_specs = (
        P(("comp", "lev"), None, "tile"),
        P(None, "tile"),
        P(("comp", "lev")),
        P(("comp", "lev"), None),
        P(),
        P("tile", None, None, None),
        P("tile", None),
        P("tile"),
        P(None, "tile"),
        P(None, "tile"),
        P(),
    )
    out_specs = (P(("comp", "lev"), None, "tile"), P(None, "tile"))
    return jax.shard_map(
        on_device, mesh=mesh, in_specs=in_specs, out_specs=out_specs, check_vma=False
    )
```

```python
import functools

import jax
import jax.numpy as jnp
from jax import lax
from jax.experimental import pallas as pl
from jax.experimental.pallas import tpu as pltpu
from jax.sharding import PartitionSpec as P

REACH_MOST = 8
PIECES = 8
CHUNKS = 8
EARLY = 4
MESH = pl.DeviceIdType.MESH
F32 = jnp.float32
BF16 = jnp.bfloat16


def iota(shape, dim):
    return lax.broadcasted_iota(jnp.int32, shape, dim)


def kernel(
    n_comp,
    n_tile,
    n_lev,
    state_in,
    spread_in,
    fraction_in,
    blend_in,
    share_in,
    weight_in,
    source_in,
    used_in,
    water_top_in,
    pond_in,
    reaction_in,
    out_state,
    out_water,
    state,
    spread,
    fraction,
    blend,
    share,
    weight,
    source,
    used,
    water,
    pond,
    reaction,
    load_sem,
    edge,
    edge_in,
    patch,
    patch_turned,
    turned,
    gathered,
    mixed,
    emission,
    part,
    part_in,
    near,
    water_in,
    ocean,
    ocean_in,
    edge_send,
    edge_recv,
    patch_send,
    patch_recv,
    lev_send,
    lev_recv,
    comp_send,
    comp_recv,
    part_send,
    part_recv,
    near_send,
    near_recv,
    water_send,
    water_recv,
    ocean_send,
    ocean_recv,
):
    depth, rows, width = state.shape
    levels = blend.shape[1]
    fields = share.shape[0]
    most = weight.shape[1]
    reach = min(REACH_MOST, (n_tile - 1) // 2)
    half = rows // n_comp
    span = rows // CHUNKS
    per_piece = depth // PIECES
    piece_rows = per_piece * rows

    comp = lax.axis_index("comp")
    tile = lax.axis_index("tile")
    lev = lax.axis_index("lev")
    block = comp * n_lev + lev
    half_at = pl.multiple_of(comp * half, half)

    def at(dc=0, dt=0, dl=0):
        return (
            lax.rem(comp + dc, n_comp),
            lax.rem(tile + dt + n_tile, n_tile),
            lax.rem(lev + dl, n_lev),
        )

    group = [(dc, dl) for dc in range(n_comp) for dl in range(n_lev) if dc or dl]
    offsets = [o for d in range(1, reach + 1) for o in (d, -d)]

    def remote(src, dst, send, recv, device):
        copy = pltpu.make_async_remote_copy(
            src_ref=src,
            dst_ref=dst,
            send_sem=send,
            recv_sem=recv,
            device_id=device,
            device_id_type=MESH,
        )
        return copy

    loads = {}
    for i, (name, src, dst) in enumerate(
        (
            ("state", state_in, state),
            ("share", share_in, share),
            ("reaction", reaction_in, reaction),
            ("spread", spread_in, spread),
            ("fraction", fraction_in, fraction),
            ("water", water_top_in, water),
            ("blend", blend_in, blend),
            ("weight", weight_in, weight),
            ("source", source_in, source),
            ("used", used_in, used),
            ("pond", pond_in, pond),
        )
    ):
        loads[name] = pltpu.make_async_copy(src, dst, load_sem.at[i])
        loads[name].start()

    barrier = pltpu.get_barrier_semaphore()
    for dc, dl in group:
        pl.semaphore_signal(barrier, inc=1, device_id=at(dc, 0, dl), device_id_type=MESH)
    for o in offsets:
        pl.semaphore_signal(barrier, inc=1, device_id=at(0, o, 0), device_id_type=MESH)

    loads["state"].wait()
    row16, col16 = iota((16, width), 0), iota((16, width), 1)
    first, last = col16 == 0, col16 == width - 1

    def pack(cells):
        packed = jnp.zeros((16, piece_rows), F32)
        for p in range(PIECES):
            pick = ((row16 == p) & last) | ((row16 == PIECES + p) & first)
            packed += lax.dot_general(
                jnp.where(pick, 1.0, 0.0).astype(BF16),
                cells(p),
                (((1,), (1,)), ((), ())),
                preferred_element_type=F32,
            )
        return packed.astype(BF16)

    edge[...] = pack(
        lambda p: state[p * per_piece : (p + 1) * per_piece].reshape(piece_rows, width)
    )

    loads["spread"].wait()
    loads["fraction"].wait()
    lat, lon = iota((rows, width), 0), iota((rows, width), 1)
    inside = (lon > 0) & (lon < width - 1)
    rate = spread[...]

    def step(k, west_edge, east_edge):
        field = state[k].astype(F32)
        west, east = pltpu.roll(field, 1, 1), pltpu.roll(field, width - 1, 1)
        if west_edge is not None:
            west = jnp.where(lon == 0, west_edge, west)
            east = jnp.where(lon == width - 1, east_edge, east)
        above = jnp.where(lat == rows - 1, 0.0, pltpu.roll(field, rows - 1, 0))
        below = jnp.where(lat == 0, 0.0, pltpu.roll(field, 1, 0))
        lap = above + below + east + west - 4.0 * field
        return field + rate * lap - fraction[k] * (field - west)

    def inner_piece(p, carry):
        for q in range(per_piece):
            k = p * per_piece + q
            moved = jnp.where(inside, step(k, None, None), 0.0)
            turned[pl.ds(k, rows, stride=depth), :] = moved
        return carry

    lax.fori_loop(0, PIECES, inner_piece, 0)
    for i in range(CHUNKS):
        lines = turned[i * span * depth : (i + 1) * span * depth]
        gathered[block, i * span : (i + 1) * span] = lines.astype(BF16).reshape(span, depth, width)

    loads["share"].wait()
    loads["reaction"].wait()
    own = iota((depth, levels), 1) == iota((depth, levels), 0) + block * depth
    own_share = lax.dot_general(
        jnp.where(own, 1.0, 0.0).astype(BF16),
        share[...],
        (((1,), (1,)), ((), ())),
        preferred_element_type=F32,
    )
    total = jnp.zeros((depth, 1), F32)
    for f in range(fields):
        total += reaction[f] * own_share[:, f : f + 1]
    emission[...] = jnp.broadcast_to(total, (depth, width))

    loads["water"].wait()
    pl.semaphore_wait(barrier, len(group) + len(offsets))

    edge_copies = []
    for s, o in enumerate((1, -1)):
        copy = remote(edge, edge_in.at[s], edge_send.at[s], edge_recv.at[s], at(0, o, 0))
        copy.start()
        edge_copies.append(copy)
    lev_copies, comp_copies = {}, {}
    def send_chunk(i):
        mine = gathered.at[block, pl.ds(i * span, span)]
        for dl in range(1, n_lev):
            copy = remote(
                mine, mine, lev_send.at[dl - 1, i], lev_recv.at[dl - 1, i], at(0, 0, dl)
            )
            copy.start()
            lev_copies[dl, i] = copy
        for dc in range(1, n_comp):
            copy = remote(
                mine, mine, comp_send.at[dc - 1, 0, i], comp_recv.at[dc - 1, 0, i], at(dc, 0, 0)
            )
            copy.start()
            comp_copies[dc, 0, i] = copy

    water_copies = []
    for s, o in enumerate((1, -1)):
        copy = remote(
            water.at[pl.ds(half_at, half)],
            water_in.at[s],
            water_send.at[s],
            water_recv.at[s],
            at(0, o, 0),
        )
        copy.start()
        water_copies.append(copy)

    for i in range(EARLY):
        send_chunk(i)

    for copy in edge_copies:
        copy.wait_recv()

    sides = jnp.concatenate([edge_in[0], edge_in[1]], axis=0).astype(F32)
    sides = sides.T.astype(BF16)
    row32, col32 = iota((32, width), 0), iota((32, width), 1)

    def one_piece(p, emitted):
        place = ((row32 == p) & (col32 == 0)) | (
            (row32 == 16 + PIECES + p) & (col32 == width - 1)
        )
        border = jnp.dot(
            sides, jnp.where(place, 1.0, 0.0).astype(BF16), preferred_element_type=F32
        )
        for q in range(per_piece):
            k = p * per_piece + q
            rim = border[q * rows : (q + 1) * rows]
            moved = step(k, rim, rim).astype(BF16).astype(F32)
            turned[pl.ds(k, rows, stride=depth), :] = moved
            emitted = emitted + emission[pl.ds(k, 1), :] * moved
        return emitted

    part[...] = lax.fori_loop(0, PIECES, one_piece, jnp.zeros((rows, width), F32))

    part_copies = []
    for i, (dc, dl) in enumerate(group):
        device = at(dc, 0, dl)
        begin = pl.multiple_of(device[0] * half, half)
        copy = remote(
            part.at[pl.ds(begin, half)], part_in.at[i], part_send.at[i], part_recv.at[i], device
        )
        copy.start()
        part_copies.append(copy)

    patch[block] = pack(
        lambda p: turned[p * piece_rows : (p + 1) * piece_rows].astype(BF16)
    )
    patch_copies = []
    for i, (dc, dl) in enumerate(group):
        copy = remote(
            patch.at[block], patch.at[block], patch_send.at[i], patch_recv.at[i], at(dc, 0, dl)
        )
        copy.start()
        patch_copies.append(copy)

    for i in range(EARLY, CHUNKS):
        send_chunk(i)
    for copy in part_copies:
        copy.wait_recv()
    flux = part[pl.ds(half_at, half), :]
    for i in range(len(group)):
        flux += part_in[i]
    near[reach] = flux.astype(BF16)
    near_copies = []
    for i, o in enumerate(offsets):
        copy = remote(
            near.at[reach], near.at[reach - o], near_send.at[i], near_recv.at[i], at(0, o, 0)
        )
        copy.start()
        near_copies.append(copy)

    def relay(i):
        for dl in range(1, n_lev):
            lev_copies[dl, i].wait_recv()
            origin = comp * n_lev + lax.rem(lev - dl + n_lev, n_lev)
            theirs = gathered.at[origin, pl.ds(i * span, span)]
            for dc in range(1, n_comp):
                copy = remote(
                    theirs,
                    theirs,
                    comp_send.at[dc - 1, dl, i],
                    comp_recv.at[dc - 1, dl, i],
                    at(dc, 0, 0),
                )
                copy.start()
                comp_copies[dc, dl, i] = copy

    def mix(i):
        for dc in range(1, n_comp):
            for dl in range(n_lev):
                comp_copies[dc, dl, i].wait_recv()
        factor = blend[...]
        place = ((row16 == i) & last) | ((row16 == PIECES + i) & first)
        place = jnp.where(place, 1.0, 0.0).astype(BF16)
        parts = []
        for b in range(n_comp * n_lev):
            rim = jnp.dot(patch_turned[b], place, preferred_element_type=F32).astype(BF16)
            parts.append(gathered[b, i * span : (i + 1) * span].reshape(piece_rows, width) + rim)
        for r in range(span):
            lines = slice(r * depth, (r + 1) * depth)
            column = jnp.concatenate([part[lines] for part in parts], axis=0)
            new = jnp.dot(factor, column, preferred_element_type=F32)
            line = i * span + r
            new += turned[line * depth : (line + 1) * depth]
            mixed[pl.ds(line, depth, stride=rows), :] = new
        done = mixed[...].reshape(depth, rows, width)[:, i * span : (i + 1) * span]
        out_state[:, i * span : (i + 1) * span, :] = done.astype(BF16)

    def remap():
        for copy in near_copies:
            copy.wait_recv()
        for copy in water_copies:
            copy.wait_recv()
        picked = []
        for b in range(most):
            slot = lax.rem(source[0, b] - tile + reach + 2 * n_tile, n_tile)
            slot = jnp.minimum(slot, 2 * reach)
            live = jnp.where(b < used[0], 1.0, 0.0).astype(F32)
            picked.append((near[slot].astype(F32) * live).astype(BF16))
        push = jnp.dot(
            jnp.concatenate(picked, axis=1),
            weight[0].reshape(most * width, width),
            preferred_element_type=F32,
        )
        top = water[...]
        above = jnp.where(lat == rows - 1, 0.0, pltpu.roll(top, rows - 1, 0))
        below = jnp.where(lat == 0, 0.0, pltpu.roll(top, 1, 0))
        ocean[...] = above + below - 4.0 * top
        mine = water[pl.ds(half_at, half), :]
        at_lon = iota((half, width), 1)
        west = jnp.where(at_lon == 0, pltpu.roll(water_in[0], 1, 1), pltpu.roll(mine, 1, 1))
        east = jnp.where(
            at_lon == width - 1,
            pltpu.roll(water_in[1], width - 1, 1),
            pltpu.roll(mine, width - 1, 1),
        )
        bend = ocean[pl.ds(half_at, half), :] + west + east
        later = mine + pond[pl.ds(half_at, half), :] * bend + push
        ocean_in[0] = later
        out_water[pl.ds(half_at, half), :] = later
        sent = []
        for dc in range(1, n_comp):
            copy = remote(
                ocean_in.at[0],
                ocean_in.at[dc],
                ocean_send.at[dc - 1],
                ocean_recv.at[dc - 1],
                at(dc, 0, 0),
            )
            copy.start()
            sent.append(copy)
        return sent

    for name in ("blend", "weight", "source", "used", "pond"):
        loads[name].wait()
    relay(0)
    relay(1)
    for copy in patch_copies:
        copy.wait_recv()
    for b in range(n_comp * n_lev):
        patch_turned[b] = patch[b].astype(F32).T.astype(BF16)
    relay(2)
    mix(0)
    relay(3)
    mix(1)
    ocean_copies = remap()
    for i in range(4, CHUNKS):
        relay(i)
        mix(i - 2)
    mix(CHUNKS - 2)
    mix(CHUNKS - 1)
    for dc in range(1, n_comp):
        ocean_copies[dc - 1].wait_recv()
        begin = pl.multiple_of(lax.rem(comp - dc + n_comp, n_comp) * half, half)
        out_water[pl.ds(begin, half), :] = ocean_in[dc]

    for copy in edge_copies + patch_copies + part_copies + water_copies + near_copies + ocean_copies:
        copy.wait_send()
    for copy in list(lev_copies.values()) + list(comp_copies.values()):
        copy.wait_send()


def solution(mesh):
    n_comp, n_tile, n_lev = (mesh.shape[a] for a in ("comp", "tile", "lev"))

    def on_device(*args):
        state, spread, fraction, blend, share, weight, source, used, water, pond, reaction = args
        depth, rows, width = state.shape
        reach = min(REACH_MOST, (n_tile - 1) // 2)
        half = rows // n_comp
        peers = n_comp * n_lev - 1
        dma = pltpu.SemaphoreType.DMA
        vmem = pl.BlockSpec(memory_space=pltpu.VMEM)
        piece = depth * rows // PIECES
        return pl.pallas_call(
            functools.partial(kernel, n_comp, n_tile, n_lev),
            out_shape=(
                jax.ShapeDtypeStruct(state.shape, state.dtype),
                jax.ShapeDtypeStruct(water.shape, water.dtype),
            ),
            in_specs=[pl.BlockSpec(memory_space=pltpu.HBM)] * len(args),
            out_specs=(vmem, vmem),
            scratch_shapes=[
                *(
                    (pltpu.SMEM if arg.ndim == 1 or arg.dtype == jnp.int32 else pltpu.VMEM)(
                        arg.shape, arg.dtype
                    )
                    for arg in args
                ),
                dma((len(args),)),
                pltpu.VMEM((16, piece), BF16),
                pltpu.VMEM((2, 16, piece), BF16),
                pltpu.VMEM((peers + 1, 16, piece), BF16),
                pltpu.VMEM((peers + 1, piece, 16), BF16),
                pltpu.VMEM((rows * depth, width), F32),
                pltpu.VMEM((n_comp * n_lev, rows, depth, width), BF16),
                pltpu.VMEM((depth * rows, width), F32),
                pltpu.VMEM((depth, width), F32),
                pltpu.VMEM((rows, width), F32),
                pltpu.VMEM((peers, half, width), F32),
                pltpu.VMEM((2 * reach + 1, half, width), BF16),
                pltpu.VMEM((2, half, width), F32),
                pltpu.VMEM((rows, width), F32),
                pltpu.VMEM((n_comp, half, width), F32),
                dma((2,)),
                dma((2,)),
                dma((peers,)),
                dma((peers,)),
                dma((n_lev - 1, CHUNKS)),
                dma((n_lev - 1, CHUNKS)),
                dma((n_comp - 1, n_lev, CHUNKS)),
                dma((n_comp - 1, n_lev, CHUNKS)),
                dma((peers,)),
                dma((peers,)),
                dma((2 * reach,)),
                dma((2 * reach,)),
                dma((2,)),
                dma((2,)),
                dma((n_comp - 1,)),
                dma((n_comp - 1,)),
            ],
            compiler_params=pltpu.CompilerParams(
                collective_id=0, has_side_effects=True, vmem_limit_bytes=63 * 1024 * 1024
            ),
            cost_estimate=pl.CostEstimate(
                flops=200_000_000, bytes_accessed=2_000_000, transcendentals=0
            ),
        )(state, spread, fraction, blend, share, weight, source, used, water, pond, reaction)

    in_specs = (
        P(("comp", "lev"), None, "tile"),
        P(None, "tile"),
        P(("comp", "lev")),
        P(("comp", "lev"), None),
        P(),
        P("tile", None, None, None),
        P("tile", None),
        P("tile"),
        P(None, "tile"),
        P(None, "tile"),
        P(),
    )
    out_specs = (P(("comp", "lev"), None, "tile"), P(None, "tile"))
    return jax.shard_map(
        on_device, mesh=mesh, in_specs=in_specs, out_specs=out_specs, check_vma=False
    )
```

```python
import functools

import jax
import jax.numpy as jnp
from jax import lax
from jax.experimental import pallas as pl
from jax.experimental.pallas import tpu as pltpu
from jax.sharding import PartitionSpec as P

REACH_MOST = 8
PIECES = 8
CHUNKS = 8
EARLY = 4
MESH = pl.DeviceIdType.MESH
F32 = jnp.float32
BF16 = jnp.bfloat16


def iota(shape, dim):
    return lax.broadcasted_iota(jnp.int32, shape, dim)


def kernel(
    n_comp,
    n_tile,
    n_lev,
    state_in,
    spread_in,
    fraction_in,
    blend_in,
    share_in,
    weight_in,
    source_in,
    used_in,
    water_top_in,
    pond_in,
    reaction_in,
    out_state,
    out_water,
    state,
    spread,
    fraction,
    blend,
    share,
    weight,
    source,
    used,
    water,
    pond,
    reaction,
    load_sem,
    edge,
    edge_in,
    patch,
    patch_turned,
    turned,
    gathered,
    mixed,
    emission,
    part,
    part_in,
    near,
    water_in,
    ocean,
    ocean_in,
    edge_send,
    edge_recv,
    patch_send,
    patch_recv,
    lev_send,
    lev_recv,
    comp_send,
    comp_recv,
    part_send,
    part_recv,
    near_send,
    near_recv,
    water_send,
    water_recv,
    ocean_send,
    ocean_recv,
):
    depth, rows, width = state.shape
    levels = blend.shape[1]
    fields = share.shape[0]
    most = weight.shape[1]
    reach = min(REACH_MOST, (n_tile - 1) // 2)
    half = rows // n_comp
    span = rows // CHUNKS
    per_piece = depth // PIECES
    piece_rows = per_piece * rows

    comp = lax.axis_index("comp")
    tile = lax.axis_index("tile")
    lev = lax.axis_index("lev")
    block = comp * n_lev + lev
    half_at = pl.multiple_of(comp * half, half)

    def at(dc=0, dt=0, dl=0):
        return (
            lax.rem(comp + dc, n_comp),
            lax.rem(tile + dt + n_tile, n_tile),
            lax.rem(lev + dl, n_lev),
        )

    group = [(dc, dl) for dc in range(n_comp) for dl in range(n_lev) if dc or dl]
    offsets = [o for d in range(1, reach + 1) for o in (d, -d)]

    def remote(src, dst, send, recv, device):
        copy = pltpu.make_async_remote_copy(
            src_ref=src,
            dst_ref=dst,
            send_sem=send,
            recv_sem=recv,
            device_id=device,
            device_id_type=MESH,
        )
        return copy

    loads = {}
    for i, (name, src, dst) in enumerate(
        (
            ("state", state_in, state),
            ("share", share_in, share),
            ("reaction", reaction_in, reaction),
            ("spread", spread_in, spread),
            ("fraction", fraction_in, fraction),
            ("water", water_top_in, water),
            ("blend", blend_in, blend),
            ("weight", weight_in, weight),
            ("source", source_in, source),
            ("used", used_in, used),
            ("pond", pond_in, pond),
        )
    ):
        loads[name] = pltpu.make_async_copy(src, dst, load_sem.at[i])
        loads[name].start()

    barrier = pltpu.get_barrier_semaphore()
    for dc, dl in group:
        pl.semaphore_signal(barrier, inc=1, device_id=at(dc, 0, dl), device_id_type=MESH)
    for o in offsets:
        pl.semaphore_signal(barrier, inc=1, device_id=at(0, o, 0), device_id_type=MESH)

    loads["state"].wait()
    row16, col16 = iota((16, width), 0), iota((16, width), 1)
    first, last = col16 == 0, col16 == width - 1

    def pack(cells):
        packed = jnp.zeros((16, piece_rows), F32)
        for p in range(PIECES):
            pick = ((row16 == p) & last) | ((row16 == PIECES + p) & first)
            packed += lax.dot_general(
                jnp.where(pick, 1.0, 0.0).astype(BF16),
                cells(p),
                (((1,), (1,)), ((), ())),
                preferred_element_type=F32,
            )
        return packed.astype(BF16)

    edge[...] = pack(
        lambda p: state[p * per_piece : (p + 1) * per_piece].reshape(piece_rows, width)
    )

    loads["spread"].wait()
    loads["fraction"].wait()
    lat, lon = iota((rows, width), 0), iota((rows, width), 1)
    inside = (lon > 0) & (lon < width - 1)
    rate = spread[...]

    def step(k, west_edge, east_edge):
        field = state[k].astype(F32)
        west, east = pltpu.roll(field, 1, 1), pltpu.roll(field, width - 1, 1)
        if west_edge is not None:
            west = jnp.where(lon == 0, west_edge, west)
            east = jnp.where(lon == width - 1, east_edge, east)
        above = jnp.where(lat == rows - 1, 0.0, pltpu.roll(field, rows - 1, 0))
        below = jnp.where(lat == 0, 0.0, pltpu.roll(field, 1, 0))
        lap = above + below + east + west - 4.0 * field
        return field + rate * lap - fraction[k] * (field - west)

    def inner_piece(p, carry):
        for q in range(per_piece):
            k = p * per_piece + q
            moved = jnp.where(inside, step(k, None, None), 0.0)
            turned[pl.ds(k, rows, stride=depth), :] = moved
        return carry

    lax.fori_loop(0, PIECES, inner_piece, 0)
    for i in range(CHUNKS):
        lines = turned[i * span * depth : (i + 1) * span * depth]
        gathered[block, i * span : (i + 1) * span] = lines.astype(BF16).reshape(span, depth, width)

    loads["share"].wait()
    loads["reaction"].wait()
    own = iota((depth, levels), 1) == iota((depth, levels), 0) + block * depth
    own_share = lax.dot_general(
        jnp.where(own, 1.0, 0.0).astype(BF16),
        share[...],
        (((1,), (1,)), ((), ())),
        preferred_element_type=F32,
    )
    total = jnp.zeros((depth, 1), F32)
    for f in range(fields):
        total += reaction[f] * own_share[:, f : f + 1]
    emission[...] = jnp.broadcast_to(total, (depth, width))

    loads["water"].wait()
    pl.semaphore_wait(barrier, len(group) + len(offsets))

    edge_copies = []
    for s, o in enumerate((1, -1)):
        copy = remote(edge, edge_in.at[s], edge_send.at[s], edge_recv.at[s], at(0, o, 0))
        copy.start()
        edge_copies.append(copy)
    lev_copies, comp_copies = {}, {}
    def send_chunk(i):
        mine = gathered.at[block, pl.ds(i * span, span)]
        for dl in range(1, n_lev):
            copy = remote(
                mine, mine, lev_send.at[dl - 1, i], lev_recv.at[dl - 1, i], at(0, 0, dl)
            )
            copy.start()
            lev_copies[dl, i] = copy
        for dc in range(1, n_comp):
            copy = remote(
                mine, mine, comp_send.at[dc - 1, 0, i], comp_recv.at[dc - 1, 0, i], at(dc, 0, 0)
            )
            copy.start()
            comp_copies[dc, 0, i] = copy

    water_copies = []
    for s, o in enumerate((1, -1)):
        copy = remote(
            water.at[pl.ds(half_at, half)],
            water_in.at[s],
            water_send.at[s],
            water_recv.at[s],
            at(0, o, 0),
        )
        copy.start()
        water_copies.append(copy)

    for i in range(EARLY):
        send_chunk(i)

    for copy in edge_copies:
        copy.wait_recv()

    sides = jnp.concatenate([edge_in[0], edge_in[1]], axis=0).astype(F32)
    sides = sides.T.astype(BF16)
    row32, col32 = iota((32, width), 0), iota((32, width), 1)

    def one_piece(p, emitted):
        place = ((row32 == p) & (col32 == 0)) | (
            (row32 == 16 + PIECES + p) & (col32 == width - 1)
        )
        border = jnp.dot(
            sides, jnp.where(place, 1.0, 0.0).astype(BF16), preferred_element_type=F32
        )
        for q in range(per_piece):
            k = p * per_piece + q
            rim = border[q * rows : (q + 1) * rows]
            moved = step(k, rim, rim).astype(BF16).astype(F32)
            turned[pl.ds(k, rows, stride=depth), :] = moved
            emitted = emitted + emission[pl.ds(k, 1), :] * moved
        return emitted

    part[...] = lax.fori_loop(0, PIECES, one_piece, jnp.zeros((rows, width), F32))

    part_copies = []
    for i, (dc, dl) in enumerate(group):
        device = at(dc, 0, dl)
        begin = pl.multiple_of(device[0] * half, half)
        copy = remote(
            part.at[pl.ds(begin, half)], part_in.at[i], part_send.at[i], part_recv.at[i], device
        )
        copy.start()
        part_copies.append(copy)

    patch[block] = pack(
        lambda p: turned[p * piece_rows : (p + 1) * piece_rows].astype(BF16)
    )
    patch_copies = []
    for i, (dc, dl) in enumerate(group):
        copy = remote(
            patch.at[block], patch.at[block], patch_send.at[i], patch_recv.at[i], at(dc, 0, dl)
        )
        copy.start()
        patch_copies.append(copy)

    for i in range(EARLY, CHUNKS):
        send_chunk(i)
    for copy in part_copies:
        copy.wait_recv()
    flux = part[pl.ds(half_at, half), :]
    for i in range(len(group)):
        flux += part_in[i]
    near[reach] = flux.astype(BF16)
    near_copies = []
    for i, o in enumerate(offsets):
        copy = remote(
            near.at[reach], near.at[reach - o], near_send.at[i], near_recv.at[i], at(0, o, 0)
        )
        copy.start()
        near_copies.append(copy)

    def relay(i):
        for dl in range(1, n_lev):
            lev_copies[dl, i].wait_recv()
            origin = comp * n_lev + lax.rem(lev - dl + n_lev, n_lev)
            theirs = gathered.at[origin, pl.ds(i * span, span)]
            for dc in range(1, n_comp):
                copy = remote(
                    theirs,
                    theirs,
                    comp_send.at[dc - 1, dl, i],
                    comp_recv.at[dc - 1, dl, i],
                    at(dc, 0, 0),
                )
                copy.start()
                comp_copies[dc, dl, i] = copy

    def mix(i):
        for dc in range(1, n_comp):
            for dl in range(n_lev):
                comp_copies[dc, dl, i].wait_recv()
        factor = blend[...]
        place = ((row16 == i) & last) | ((row16 == PIECES + i) & first)
        place = jnp.where(place, 1.0, 0.0).astype(BF16)
        parts = []
        for b in range(n_comp * n_lev):
            rim = jnp.dot(patch_turned[b], place, preferred_element_type=F32).astype(BF16)
            parts.append(gathered[b, i * span : (i + 1) * span].reshape(piece_rows, width) + rim)
        for r in range(span):
            lines = slice(r * depth, (r + 1) * depth)
            column = jnp.concatenate([part[lines] for part in parts], axis=0)
            new = jnp.dot(factor, column, preferred_element_type=F32)
            line = i * span + r
            new += turned[line * depth : (line + 1) * depth]
            mixed[pl.ds(line, depth, stride=rows), :] = new
        done = mixed[...].reshape(depth, rows, width)[:, i * span : (i + 1) * span]
        out_state[:, i * span : (i + 1) * span, :] = done.astype(BF16)

    def remap():
        for copy in near_copies:
            copy.wait_recv()
        for copy in water_copies:
            copy.wait_recv()
        picked = []
        for b in range(most):
            slot = lax.rem(source[0, b] - tile + reach + 2 * n_tile, n_tile)
            slot = jnp.minimum(slot, 2 * reach)
            live = jnp.where(b < used[0], 1.0, 0.0).astype(F32)
            picked.append((near[slot].astype(F32) * live).astype(BF16))
        push = jnp.dot(
            jnp.concatenate(picked, axis=1),
            weight[0].reshape(most * width, width),
            preferred_element_type=F32,
        )
        top = water[...]
        above = jnp.where(lat == rows - 1, 0.0, pltpu.roll(top, rows - 1, 0))
        below = jnp.where(lat == 0, 0.0, pltpu.roll(top, 1, 0))
        ocean[...] = above + below - 4.0 * top
        mine = water[pl.ds(half_at, half), :]
        at_lon = iota((half, width), 1)
        west = jnp.where(at_lon == 0, pltpu.roll(water_in[0], 1, 1), pltpu.roll(mine, 1, 1))
        east = jnp.where(
            at_lon == width - 1,
            pltpu.roll(water_in[1], width - 1, 1),
            pltpu.roll(mine, width - 1, 1),
        )
        bend = ocean[pl.ds(half_at, half), :] + west + east
        later = mine + pond[pl.ds(half_at, half), :] * bend + push
        ocean_in[0] = later
        out_water[pl.ds(half_at, half), :] = later
        sent = []
        for dc in range(1, n_comp):
            copy = remote(
                ocean_in.at[0],
                ocean_in.at[dc],
                ocean_send.at[dc - 1],
                ocean_recv.at[dc - 1],
                at(dc, 0, 0),
            )
            copy.start()
            sent.append(copy)
        return sent

    for name in ("blend", "weight", "source", "used", "pond"):
        loads[name].wait()
    relay(0)
    relay(1)
    for copy in patch_copies:
        copy.wait_recv()
    for b in range(n_comp * n_lev):
        patch_turned[b] = patch[b].astype(F32).T.astype(BF16)
    relay(2)
    mix(0)
    relay(3)
    mix(1)
    for i in range(4, CHUNKS):
        relay(i)
        mix(i - 2)
        if i == 5:
            ocean_copies = remap()
    mix(CHUNKS - 2)
    mix(CHUNKS - 1)
    for dc in range(1, n_comp):
        ocean_copies[dc - 1].wait_recv()
        begin = pl.multiple_of(lax.rem(comp - dc + n_comp, n_comp) * half, half)
        out_water[pl.ds(begin, half), :] = ocean_in[dc]

    for copy in edge_copies + patch_copies + part_copies + water_copies + near_copies + ocean_copies:
        copy.wait_send()
    for copy in list(lev_copies.values()) + list(comp_copies.values()):
        copy.wait_send()


def solution(mesh):
    n_comp, n_tile, n_lev = (mesh.shape[a] for a in ("comp", "tile", "lev"))

    def on_device(*args):
        state, spread, fraction, blend, share, weight, source, used, water, pond, reaction = args
        depth, rows, width = state.shape
        reach = min(REACH_MOST, (n_tile - 1) // 2)
        half = rows // n_comp
        peers = n_comp * n_lev - 1
        dma = pltpu.SemaphoreType.DMA
        vmem = pl.BlockSpec(memory_space=pltpu.VMEM)
        piece = depth * rows // PIECES
        return pl.pallas_call(
            functools.partial(kernel, n_comp, n_tile, n_lev),
            out_shape=(
                jax.ShapeDtypeStruct(state.shape, state.dtype),
                jax.ShapeDtypeStruct(water.shape, water.dtype),
            ),
            in_specs=[pl.BlockSpec(memory_space=pltpu.HBM)] * len(args),
            out_specs=(vmem, vmem),
            scratch_shapes=[
                *(
                    (pltpu.SMEM if arg.ndim == 1 or arg.dtype == jnp.int32 else pltpu.VMEM)(
                        arg.shape, arg.dtype
                    )
                    for arg in args
                ),
                dma((len(args),)),
                pltpu.VMEM((16, piece), BF16),
                pltpu.VMEM((2, 16, piece), BF16),
                pltpu.VMEM((peers + 1, 16, piece), BF16),
                pltpu.VMEM((peers + 1, piece, 16), BF16),
                pltpu.VMEM((rows * depth, width), F32),
                pltpu.VMEM((n_comp * n_lev, rows, depth, width), BF16),
                pltpu.VMEM((depth * rows, width), F32),
                pltpu.VMEM((depth, width), F32),
                pltpu.VMEM((rows, width), F32),
                pltpu.VMEM((peers, half, width), F32),
                pltpu.VMEM((2 * reach + 1, half, width), BF16),
                pltpu.VMEM((2, half, width), F32),
                pltpu.VMEM((rows, width), F32),
                pltpu.VMEM((n_comp, half, width), F32),
                dma((2,)),
                dma((2,)),
                dma((peers,)),
                dma((peers,)),
                dma((n_lev - 1, CHUNKS)),
                dma((n_lev - 1, CHUNKS)),
                dma((n_comp - 1, n_lev, CHUNKS)),
                dma((n_comp - 1, n_lev, CHUNKS)),
                dma((peers,)),
                dma((peers,)),
                dma((2 * reach,)),
                dma((2 * reach,)),
                dma((2,)),
                dma((2,)),
                dma((n_comp - 1,)),
                dma((n_comp - 1,)),
            ],
            compiler_params=pltpu.CompilerParams(
                collective_id=0, has_side_effects=True, vmem_limit_bytes=63 * 1024 * 1024
            ),
            cost_estimate=pl.CostEstimate(
                flops=200_000_000, bytes_accessed=2_000_000, transcendentals=0
            ),
        )(state, spread, fraction, blend, share, weight, source, used, water, pond, reaction)

    in_specs = (
        P(("comp", "lev"), None, "tile"),
        P(None, "tile"),
        P(("comp", "lev")),
        P(("comp", "lev"), None),
        P(),
        P("tile", None, None, None),
        P("tile", None),
        P("tile"),
        P(None, "tile"),
        P(None, "tile"),
        P(),
    )
    out_specs = (P(("comp", "lev"), None, "tile"), P(None, "tile"))
    return jax.shard_map(
        on_device, mesh=mesh, in_specs=in_specs, out_specs=out_specs, check_vma=False
    )
```
